32 devices in a mesh: wide: 8 (over z, x), narrow: 4 (over y, core).
Axes of the slice: x: 2, y: 2, z: 4, core: 2. Of those that a mesh axis runs over, the one named last changes fastest.
Arguments:
- tokens_in: bfloat16 [1024, 2560], P('wide', 'narrow'), may hold values from -6 to 6
- norm_gain: bfloat16 [2560], replicated, may hold values from 0.099609375 to 1.8984375
- query_weight: bfloat16 [2560, 2560], P('wide', 'narrow'), may hold values from -0.25 to 0.25
- key_weight: bfloat16 [2560, 640], P('wide', 'narrow'), may hold values from -0.125 to 0.125
- value_weight: bfloat16 [2560, 640], P('wide', 'narrow'), may hold values from -0.5 to 0.5
- out_weight: bfloat16 [2560, 2560], P('wide', 'narrow'), may hold values from -0.125 to 0.125
- cache_keys: bfloat16 [640, 8192], P('narrow', 'wide'), may hold values from -64 to 64
- cache_values: bfloat16 [640, 8192], P('narrow', 'wide'), may hold values from -24 to 24
- cached_len: int32 [2], replicated, may hold values from 1 to 4096, as said below
- append_slot: int32 [2], replicated, may hold values from 0 to 4095
- shard_owner: int32 [2], replicated, may hold values from 0 to 3
Outputs:
- attention_update: bfloat16 [1024, 2560], P('wide', 'narrow')
- appended_keys: bfloat16 [640, 8192], P('narrow', 'wide')
- appended_values: bfloat16 [640, 8192], P('narrow', 'wide')
The draws below stay inside these ranges and needn't reach their ends.
Inputs may be any that keep to these rules, and one draw needn't show every extreme that they name: `cached_len`: each request's number of cached keys; some request holds 4096.
All inputs are finite; a program needn't handle non-finite values.
Results may differ from the reference program's by a relative error of at most 0.012.
The reference program's roundings to bfloat16 on the way count: a program that leaves them out, or rounds other values in their place, can miss the bound.
Values may be sent and summed in bfloat16 or wider, within the bound.
No kernel may reach another device: no remote copies, remote signals or barrier semaphores. Data moves between devices by JAX's collectives and lax.ppermute only.
A program may use at most 64 MiB of HBM per device.

```python
import jax
import jax.numpy as jnp
from jax import lax

D = 2560
HEADS = 32
KV_HEADS = 8
HEAD_DIM = 80
WIN = 4096
GROUP = 4
NEW = 512
REQS = 2
TOKENS = 1024


def draw_cached_len(key, part):
    key_len, key_pick = jax.random.split(key)
    lengths = jax.random.randint(key_len, (REQS,), 1, WIN + 1)
    chosen = jax.random.randint(key_pick, (), 0, REQS)
    return jnp.where(jnp.arange(REQS) == chosen, WIN, lengths).astype(jnp.int32)


def draw_cache_keys(key, part):
    key_base = jax.random.fold_in(jax.random.fold_in(key, 11), 0)
    width = KV_HEADS * HEAD_DIM
    return jax.random.normal(key_base, (REQS * WIN, width), jnp.float32).T.astype(jnp.bfloat16)


def steps_of(rng, shape, cuts, low, high):
    def one(dim, blocks):
        heights = jax.random.uniform(jax.random.fold_in(jax.random.fold_in(rng, 6), dim), (blocks,), jnp.float32, low / len(cuts), high / len(cuts))
        return jnp.repeat(jnp.exp(heights), shape[dim] // blocks).reshape((-1,) + (1,) * (len(shape) - dim - 1))

    level = one(*cuts[0])
    for cut in cuts[1:]:
        level = level * one(*cut)
    return level


def scatter_about(key, dims, deviation, reach, cuts=(), kind=jnp.bfloat16):
    values = deviation * jax.random.normal(key, dims, jnp.float32)
    if cuts:
        values = values * steps_of(key, dims, cuts, -0.22, 0.18)
    return jnp.clip(values, -reach, reach).astype(kind)


def setup_inputs(seed: int = 0) -> dict:
    arg_keys = jax.random.split(jax.random.key(seed), 12)
    return {
        "tokens_in": scatter_about(arg_keys[0], (TOKENS, D), 1.0, 6.0, ((0, 8), (1, 4))),
        "norm_gain": jnp.clip(1.0 + 0.18 * jax.random.normal(arg_keys[1], (D,), jnp.float32), 0.099609375, 1.8984375).astype(jnp.bfloat16),
        "query_weight": scatter_about(arg_keys[2], (D, HEADS * HEAD_DIM), (D // 4) ** -0.5, 0.25, ((0, 8), (1, 4))),
        "key_weight": scatter_about(arg_keys[3], (D, KV_HEADS * HEAD_DIM), D ** -0.5, 0.125, ((0, 8), (1, 4))),
        "value_weight": scatter_about(arg_keys[4], (D, KV_HEADS * HEAD_DIM), (D // 16) ** -0.5, 0.5, ((0, 8), (1, 4))),
        "out_weight": scatter_about(arg_keys[5], (HEADS * HEAD_DIM, D), (HEADS * HEAD_DIM) ** -0.5, 0.125, ((0, 8), (1, 4))),
        "cache_keys": draw_cache_keys(jax.random.fold_in(arg_keys[11], 71), 0),
        "cache_values": scatter_about(arg_keys[7], (KV_HEADS * HEAD_DIM, REQS * WIN), 4.0, 24.0, ((0, 4), (1, 8))),
        "cached_len": draw_cached_len(jax.random.fold_in(arg_keys[11], 71), 0),
        "append_slot": jax.random.randint(arg_keys[9], (REQS,), 0, WIN).astype(jnp.int32),
        "shard_owner": jax.random.randint(arg_keys[10], (REQS,), 0, GROUP).astype(jnp.int32),
    }


EPSILON = 1e-05
ROPE_BASE = 10000.0

def rms_normed(rows_in, gain):
    values = rows_in.astype(jnp.float32)
    scaling = lax.rsqrt(lax.optimization_barrier(jnp.mean(values * values, axis=-1, keepdims=True)) + EPSILON)
    return (values * scaling * gain.astype(jnp.float32)).astype(jnp.bfloat16)

def rotate(values, positions):
    half_dim = values.shape[-1] // 2
    inverse = ROPE_BASE ** (-(jnp.arange(half_dim, dtype=jnp.float32) * (2.0 / values.shape[-1])))
    angles = positions.astype(jnp.float32)[:, None] * inverse[None, :]
    cos_part = jnp.cos(angles)[:, None, :]
    sin_part = jnp.sin(angles)[:, None, :]
    lower = values[..., :half_dim]
    higher = values[..., half_dim:]
    return jnp.concatenate([lower * cos_part - higher * sin_part, higher * cos_part + lower * sin_part], axis=-1)

def reference(tokens_in, norm_gain, query_weight, key_weight, value_weight, out_weight, cache_keys, cache_values, cached_len, append_slot, shard_owner):
    normed = rms_normed(tokens_in, norm_gain)
    repeats = HEADS // KV_HEADS
    shard_rows = WIN // GROUP
    kv_width = KV_HEADS * HEAD_DIM
    new_steps = jnp.arange(NEW, dtype=jnp.int32)
    positions = jnp.repeat(cached_len, NEW, total_repeat_length=TOKENS) + jnp.tile(new_steps, REQS)
    query_all = jnp.dot(normed, query_weight, preferred_element_type=jnp.float32).reshape(TOKENS, HEADS, HEAD_DIM)
    query_all = rotate(query_all, positions).astype(jnp.bfloat16)
    key_all = jnp.dot(normed, key_weight, preferred_element_type=jnp.float32).reshape(TOKENS, KV_HEADS, HEAD_DIM)
    key_all = rotate(key_all, positions).astype(jnp.bfloat16).reshape(TOKENS, kv_width)
    value_all = jnp.dot(normed, value_weight, preferred_element_type=jnp.float32).astype(jnp.bfloat16)
    storage = jnp.arange(WIN, dtype=jnp.int32)
    scale = HEAD_DIM ** (-0.5)

    def per_request(request):
        length = cached_len[request]
        offset = append_slot[request]
        owner = shard_owner[request]
        cycle = (storage // shard_rows - owner) % GROUP * shard_rows + storage % shard_rows
        cached_pos = (cycle - offset + length) % WIN
        cached_ok = cached_pos < length
        first_row = (request * WIN).astype(jnp.int32)
        old_keys = lax.dynamic_slice_in_dim(cache_keys, first_row, WIN, 1).T
        old_values = lax.dynamic_slice_in_dim(cache_values, first_row, WIN, 1).T
        first_new = (request * NEW).astype(jnp.int32)
        fresh_keys = lax.dynamic_slice_in_dim(key_all, first_new, NEW, 0)
        fresh_values = lax.dynamic_slice_in_dim(value_all, first_new, NEW, 0)
        req_queries = lax.dynamic_slice_in_dim(query_all, first_new, NEW, 0)
        keys_joined = jnp.concatenate([old_keys, fresh_keys], axis=0).reshape(WIN + NEW, KV_HEADS, HEAD_DIM)
        values_joined = jnp.concatenate([old_values, fresh_values], axis=0).reshape(WIN + NEW, KV_HEADS, HEAD_DIM)
        key_pos = jnp.concatenate([cached_pos, length + new_steps])
        key_ok = jnp.concatenate([cached_ok, jnp.ones((NEW,), dtype=bool)])
        query_pos = length + new_steps
        allowed = key_ok[None, :] & (key_pos[None, :] <= query_pos[:, None]) & (query_pos[:, None] - key_pos[None, :] < WIN)

        def per_group(group):
            group_queries = lax.dynamic_slice_in_dim(req_queries, group * repeats, repeats, 1).astype(jnp.float32)
            group_keys = lax.dynamic_slice_in_dim(keys_joined, group, 1, 1)[:, 0].astype(jnp.float32)
            group_values = lax.dynamic_slice_in_dim(values_joined, group, 1, 1)[:, 0].astype(jnp.float32)
            scores = jnp.einsum('trd,kd->rtk', group_queries, group_keys) * scale
            masked = jnp.where(allowed[None], scores, -jnp.inf)
            top_score = lax.optimization_barrier(jnp.max(masked, axis=-1, keepdims=True))
            weights = jnp.exp(masked - top_score)
            total = lax.optimization_barrier(jnp.sum(weights, axis=-1))
            rounded = lax.optimization_barrier(weights.astype(jnp.bfloat16))
            mixed = jnp.einsum('rtk,kd->rtd', rounded.astype(jnp.float32), group_values)
            return mixed / total[:, :, None]
        per_head = lax.map(per_group, jnp.arange(KV_HEADS, dtype=jnp.int32))
        attended = jnp.transpose(per_head, (2, 0, 1, 3)).reshape(NEW, HEADS * HEAD_DIM).astype(jnp.bfloat16)
        new_index = (cycle - offset) % WIN
        written = new_index < NEW
        take_rows = jnp.minimum(new_index, NEW - 1)
        put_keys = jnp.where(written[:, None], fresh_keys[take_rows], old_keys)
        put_values = jnp.where(written[:, None], fresh_values[take_rows], old_values)
        return (attended, put_keys, put_values)
    attended, put_keys, put_values = lax.map(per_request, jnp.arange(REQS, dtype=jnp.int32))
    attended = attended.reshape(TOKENS, HEADS * HEAD_DIM)
    update = jnp.dot(attended, out_weight, preferred_element_type=jnp.float32).astype(jnp.bfloat16)
    return (update, put_keys.reshape(REQS * WIN, kv_width).T, put_values.reshape(REQS * WIN, kv_width).T)
```

```python
import functools
import math

import jax
import jax.numpy as jnp
from jax import lax
from jax.experimental import pallas as pl
from jax.experimental.pallas import tpu as pltpu
from jax.sharding import PartitionSpec as P

HEAD_DIM = 80
WIN = 4096
GROUP_BITS = 2
GROUP = 4


EPSILON = 1e-05
ROPE_BASE = 10000.0
LOWEST = -1e30


def from_partner(block, axis, bit):
    count = lax.axis_size(axis)
    route = []
    for low in range(count):
        high = low | 1 << bit
        if high != low and high < count:
            route += [(low, high), (high, low)]
    return lax.ppermute(block, axis, route)


def rms_normed(rows_in, gain):
    values = rows_in.astype(jnp.float32)
    scaling = lax.rsqrt(jnp.mean(values * values, axis=-1, keepdims=True) + EPSILON)
    return (values * scaling * gain.astype(jnp.float32)).astype(jnp.bfloat16)


def rotate(values, positions):
    half_dim = values.shape[-1] // 2
    inverse = ROPE_BASE ** (-(jnp.arange(half_dim, dtype=jnp.float32) * (2.0 / values.shape[-1])))
    angles = positions.astype(jnp.float32)[:, None] * inverse[None, :]
    cos_part = jnp.cos(angles)[:, None, :]
    sin_part = jnp.sin(angles)[:, None, :]
    lower = values[..., :half_dim]
    higher = values[..., half_dim:]
    return jnp.concatenate(
        [lower * cos_part - higher * sin_part, higher * cos_part + lower * sin_part], axis=-1
    )


def ordered(mine, other, upper, along):
    first_half = jnp.where(upper, other, mine)
    second_half = jnp.where(upper, mine, other)
    return jnp.concatenate([first_half, second_half], axis=along)


def empty_state(row_count, groups, repeats):
    return (
        jnp.zeros((row_count, groups, repeats, HEAD_DIM), jnp.float32),
        jnp.full((row_count, groups, repeats), LOWEST, jnp.float32),
        jnp.zeros((row_count, groups, repeats), jnp.float32),
    )


def fold_keys(state, queries, query_pos, keys, values, key_pos, key_ok, widest):
    key_count = keys.shape[1]
    groups = queries.shape[1]
    block = math.gcd(key_count, widest)
    keys_split = keys.reshape(groups, HEAD_DIM, key_count)
    values_split = values.reshape(groups, HEAD_DIM, key_count)
    scale = HEAD_DIM ** (-0.5)

    def step(index, carry):
        accum, top_old, sum_old = carry
        start = index * block
        block_keys = lax.dynamic_slice_in_dim(keys_split, start, block, 2)
        block_values = lax.dynamic_slice_in_dim(values_split, start, block, 2)
        block_pos = lax.dynamic_slice_in_dim(key_pos, start, block, 0)
        block_ok = lax.dynamic_slice_in_dim(key_ok, start, block, 0)
        scores = (
            jnp.einsum("tgrd,gdk->tgrk", queries, block_keys, preferred_element_type=jnp.float32)
            * scale
        )
        allowed = (
            block_ok[None, :]
            & (block_pos[None, :] <= query_pos[:, None])
            & (query_pos[:, None] - block_pos[None, :] < WIN)
        )
        allowed = allowed[:, None, None, :]
        top_new = jnp.maximum(top_old, jnp.max(jnp.where(allowed, scores, LOWEST), axis=-1))
        weights = jnp.where(allowed, jnp.exp(scores - top_new[..., None]), 0.0)
        rescale = jnp.exp(top_old - top_new)
        sum_new = sum_old * rescale + jnp.sum(weights, axis=-1)
        mixed = jnp.einsum(
            "tgrk,gdk->tgrd",
            weights.astype(jnp.bfloat16),
            block_values,
            preferred_element_type=jnp.float32,
        )
        return (accum * rescale[..., None] + mixed, top_new, sum_new)

    return lax.fori_loop(0, key_count // block, step, state)


def shards_any(
    tokens_in,
    norm_gain,
    query_weight,
    key_weight,
    value_weight,
    out_weight,
    cache_keys,
    cache_values,
    cached_len,
    append_slot,
    shard_owner,
):
    whole = lax.all_gather(tokens_in, "narrow", axis=1, tiled=True)
    normed = rms_normed(whole, norm_gain)
    tok_rows = whole.shape[0]
    query_width = query_weight.shape[1]
    kv_width = key_weight.shape[1]
    local_heads = query_width // HEAD_DIM
    local_groups = kv_width // HEAD_DIM
    repeats = local_heads // local_groups
    columns = normed
    query_sum = jnp.dot(
        columns,
        lax.all_gather(query_weight, "wide", axis=0, tiled=True),
        preferred_element_type=jnp.float32,
    )
    key_sum = jnp.dot(
        columns,
        lax.all_gather(key_weight, "wide", axis=0, tiled=True),
        preferred_element_type=jnp.float32,
    )
    value_sum = jnp.dot(
        columns,
        lax.all_gather(value_weight, "wide", axis=0, tiled=True),
        preferred_element_type=jnp.float32,
    )
    position = lax.axis_index("wide")
    request = position // GROUP
    place = position % GROUP
    length = cached_len[request]
    offset = append_slot[request]
    owner = shard_owner[request]
    query_pos = length + place * tok_rows + jnp.arange(tok_rows, dtype=jnp.int32)
    queries = rotate(query_sum.reshape(tok_rows, local_heads, HEAD_DIM), query_pos).astype(
        jnp.bfloat16
    )
    queries = queries.reshape(tok_rows, local_groups, repeats, HEAD_DIM)
    new_keys = (
        rotate(key_sum.reshape(tok_rows, local_groups, HEAD_DIM), query_pos)
        .astype(jnp.bfloat16)
        .reshape(tok_rows, kv_width)
    )
    new_values = value_sum.astype(jnp.bfloat16)
    shard_rows = cache_keys.shape[1]
    within = jnp.arange(shard_rows, dtype=jnp.int32)
    cycle_mine = (place - owner) % GROUP * shard_rows + within
    old_keys, old_values = (cache_keys, cache_values)
    for bit in range(GROUP_BITS):
        upper = place // 2**bit % 2 == 1
        other_keys, other_values, other_old_keys, other_old_values = from_partner(
            (new_keys, new_values, old_keys, old_values), "wide", bit
        )
        new_keys = ordered(new_keys, other_keys, upper, 0)
        new_values = ordered(new_values, other_values, upper, 0)
        old_keys = ordered(old_keys, other_old_keys, upper, 1)
        old_values = ordered(old_values, other_old_values, upper, 1)
    slot_index = jnp.arange(old_keys.shape[1], dtype=jnp.int32)
    cycle = (slot_index // shard_rows - owner) % GROUP * shard_rows + slot_index % shard_rows
    cached_pos = (cycle - offset + length) % WIN
    state = fold_keys(
        empty_state(tok_rows, local_groups, repeats),
        queries,
        query_pos,
        old_keys,
        old_values,
        cached_pos,
        cached_pos < length,
        512,
    )
    key_cols = new_keys.T
    value_cols = new_values.T
    new_count = key_cols.shape[1]
    new_pos = length + jnp.arange(new_count, dtype=jnp.int32)
    state = fold_keys(
        state,
        queries,
        query_pos,
        key_cols,
        value_cols,
        new_pos,
        jnp.ones((new_count,), dtype=bool),
        512,
    )
    accum, top_score, total = state
    attended = (accum / total[..., None]).astype(jnp.bfloat16).reshape(tok_rows, query_width)
    all_heads = lax.all_gather(attended, "narrow", axis=1, tiled=True)
    columns = all_heads
    update = jnp.dot(
        columns,
        lax.all_gather(out_weight, "wide", axis=0, tiled=True),
        preferred_element_type=jnp.float32,
    ).astype(jnp.bfloat16)
    new_index = (cycle_mine - offset) % WIN
    written = new_index < new_count
    take_rows = jnp.minimum(new_index, new_count - 1)
    put_keys = jnp.where(written[None, :], jnp.take(key_cols, take_rows, axis=1), cache_keys)
    put_values = jnp.where(written[None, :], jnp.take(value_cols, take_rows, axis=1), cache_values)
    return (update, put_keys, put_values)


F32 = jnp.float32
BF16 = jnp.bfloat16
MASKED = -1e30
FLOOR = -1e29
EXP2_SCALE = HEAD_DIM ** (-0.5) * math.log2(math.e)
CHUNK = 512
NEW = 512


def send(block, to):
    route = []
    for z in range(4):
        for x in range(2):
            for y in range(2):
                for c in range(2):
                    there = to(z, x, y, c)
                    if there is not None:
                        tz, tx, ty, tc = there
                        route.append(((2 * z + x) * 4 + 2 * y + c, (2 * tz + tx) * 4 + 2 * ty + tc))
    return lax.ppermute(block, ("wide", "narrow"), route)


def after(block, *earlier):
    return lax.optimization_barrier((block, *earlier))[0]


def call(kernel, outs, *args, scalars=0, scratch=(), flops=1):
    specs = [pl.BlockSpec(memory_space=pltpu.SMEM)] * scalars
    specs += [pl.BlockSpec(memory_space=pltpu.VMEM)] * (len(args) - scalars)
    return pl.pallas_call(
        kernel,
        out_shape=outs,
        in_specs=specs,
        out_specs=jax.tree.map(lambda _: pl.BlockSpec(memory_space=pltpu.VMEM), outs),
        scratch_shapes=scratch,
        compiler_params=pltpu.CompilerParams(vmem_limit_bytes=40 * 1024 * 1024),
        cost_estimate=pl.CostEstimate(flops=flops, bytes_accessed=1, transcendentals=0),
    )(*args)


def shaped(shape, kind=BF16):
    return jax.ShapeDtypeStruct(shape, kind)


def coordinates():
    wide = lax.axis_index("wide")
    narrow = lax.axis_index("narrow")
    return wide >> 1, wide & 1, narrow >> 1, narrow & 1


def pack_weights_kernel(wq, wk, wv, w_keep, w_give):
    z, _, _, _ = coordinates()
    zz = z & 1
    for group in range(2):

        def fill(weights, group=group):
            weights[:, 0:320] = wq[:, 320 * group : 320 * (group + 1)]
            weights[:, 320:400] = wk[80 * group : 80 * (group + 1)].T
            weights[:, 400:480] = wv[80 * group : 80 * (group + 1)].T

        @pl.when(zz == group)
        def _(fill=fill):
            fill(w_keep)

        @pl.when(zz != group)
        def _(fill=fill):
            fill(w_give)


def pack_cache_kernel(tokens, keys, values, kv_own, kv_give, squares):
    z, _, _, _ = coordinates()
    zz = z & 1
    for group in range(2):

        def fill(cache, group=group):
            cache[0:80] = keys[80 * group : 80 * (group + 1)]
            cache[80:160] = values[80 * group : 80 * (group + 1)]

        @pl.when(zz == group)
        def _(fill=fill):
            fill(kv_own)

        @pl.when(zz != group)
        def _(fill=fill):
            fill(kv_give)

    wide_tokens = tokens[...].astype(F32)
    total = jnp.sum(wide_tokens * wide_tokens, axis=1, keepdims=True)
    squares[...] = jnp.broadcast_to(total, (128, 128)).T[0:8]


def current_kernel(tokens, crossed, squares, squares_z2, out):
    z, _, y, _ = coordinates()
    at_home = y == z >> 1

    @pl.when(at_home)
    def _():
        out[0:128] = tokens[...]

    @pl.when(jnp.logical_not(at_home))
    def _():
        out[0:128] = crossed[...]

    out[128:144] = jnp.zeros((16, 640), BF16)
    row = lax.broadcasted_iota(jnp.int32, (16, 128), 0)
    rest = jnp.where(
        row == 0,
        jnp.concatenate([squares[...]] * 2, axis=0),
        jnp.where(row == 1, jnp.concatenate([squares_z2[...]] * 2, axis=0), 0.0),
    )
    for part in range(3):
        rounded = rest.astype(BF16)
        rest = rest - rounded.astype(F32)
        out[128:144, 128 * part : 128 * (part + 1)] = rounded


def pieces_kernel(weight, swapped, kv_own, here, there, joined):
    z, x, _, _ = coordinates()
    same = (z & 1) == x

    @pl.when(same)
    def _():
        here[...] = weight[0:160]
        there[...] = swapped[...]

    @pl.when(jnp.logical_not(same))
    def _():
        here[...] = swapped[...]
        there[...] = weight[0:160]

    joined[:, 0:1024] = kv_own[...]
    joined[:, 1024:1664] = here[...]


def assemble_kernel(near, far, out):
    _, x, _, _ = coordinates()
    depth = near.shape[0]
    out[pl.ds(pl.multiple_of(x * depth, 64), depth), 0:480] = near[...]
    out[pl.ds(pl.multiple_of((1 - x) * depth, 64), depth), 0:480] = far[...]
    out[:, 480:] = jnp.zeros((2 * depth, 32), BF16)


def stack_kernel(first, second, out):
    out[0] = first[...]
    out[1] = second[...]


def project_kernel(
    gain, current, from_z, from_y, from_zy, other, w_rows, w_rows_z,
    own_out, send_out
):
    z, x, y, core = coordinates()
    half, zz = z >> 1, z & 1
    at_home = y == half
    here = zz == core
    w_here = jnp.where(here, w_rows[...], w_rows_z[...])
    w_there = jnp.where(here, w_rows_z[...], w_rows[...])
    both = gain[pl.ds(half, 1)][0]
    swap = core == 1
    gain_here = jnp.where(swap, both[1:2], both[0:1])
    gain_there = jnp.where(swap, both[0:1], both[1:2])

    def stats(block):
        rows = block[128:144].astype(F32)
        return rows[:, 0:128] + rows[:, 128:256] + rows[:, 256:384]

    def scaling_of(blocks):
        total = sum(stats(block) for block in blocks)
        scale = lax.rsqrt(total / 2560.0 + EPSILON)
        return jnp.concatenate([scale] * 8, axis=0).T

    scale_z = scaling_of((current, from_y, other.at[0], other.at[2]))
    scale_z1 = scaling_of((from_z, from_zy, other.at[1], other.at[3]))

    def product(here, there, scale):
        normed_here = (here[0:128].astype(F32) * scale * gain_here).astype(BF16)
        normed_there = (there[0:128].astype(F32) * scale * gain_there).astype(BF16)
        total = jnp.dot(normed_here, w_here, preferred_element_type=F32)
        total += jnp.dot(normed_there, w_there, preferred_element_type=F32)
        return total.T[0:480]

    def products(first, second, row, out):
        for (here, there), scaling, place in (
            (first, scale_z[:, row : row + 1], zz),
            (second, scale_z1[:, row : row + 1], 1 - zz),
        ):
            result = product(here, there, scaling)
            lanes = pl.ds(pl.multiple_of(place * 128, 128), 128)
            out[:, lanes] = result.astype(out.dtype)

    first = ((current, other.at[0]), (from_z, other.at[1]))
    second = ((from_y, other.at[2]), (from_zy, other.at[3]))

    @pl.when(at_home)
    def _():
        products(*second, 1, send_out)
        products(*first, 0, own_out)

    @pl.when(jnp.logical_not(at_home))
    def _():
        products(*first, 1, send_out)
        products(*second, 0, own_out)


def rotary_kernel(own, received, cos, sin, piece_2, q_out, kv_out):
    total = own[...] + received[...].astype(F32)
    cos_part = cos[...]
    sin_part = sin[...]
    rows = own.shape[1]

    def rotated(first):
        lower = total[first : first + 40]
        higher = total[first + 40 : first + 80]
        return jnp.concatenate(
            [lower * cos_part - higher * sin_part, higher * cos_part + lower * sin_part], axis=0
        ).astype(BF16)

    for head in range(4):
        q_out[:, head * rows : (head + 1) * rows] = rotated(80 * head)
    kv_out[0:80, 0:256] = rotated(320)
    kv_out[80:160, 0:256] = total[400:480].astype(BF16)
    kv_out[:, 256:896] = piece_2[...]


def score(keys, queries, allowed, scores, first, top):
    turned = keys.T
    count = turned.shape[0]
    for head in range(4):
        lanes = slice(head * 256, (head + 1) * 256)
        part = jnp.dot(turned, queries[:, lanes], preferred_element_type=F32) * EXP2_SCALE
        if allowed is not None:
            part = jnp.where(allowed, part, MASKED)
        scores[first : first + count, lanes] = part
        top[:, lanes] = jnp.maximum(
            top[:, lanes], jnp.max(part.reshape(count // 8, 8, 256), axis=0)
        )


def weigh(scores, values_of, block, top, top_old, acc_old, total_old, acc, top_out, total):
    count = scores.shape[0]
    for head in range(4):
        lanes = slice(head * 256, (head + 1) * 256)
        best = jnp.max(top[:, lanes], axis=0, keepdims=True)
        if top_old is not None:
            best = jnp.maximum(best, top_old[0:1, lanes])
        sums = jnp.zeros((8, 256), F32)
        mixed = jnp.zeros((80, 256), F32)
        for first in range(0, count, block):
            weights = jnp.exp2(scores[first : first + block, lanes] - best)
            sums += jnp.sum(weights.reshape(block // 8, 8, 256), axis=0)
            mixed += jnp.dot(
                values_of(first), weights.astype(BF16), preferred_element_type=F32
            )
        sums = jnp.sum(sums, axis=0, keepdims=True)
        if top_old is not None:
            rescale = jnp.exp2(top_old[0:1, lanes] - best)
            sums += total_old[0:1, lanes] * rescale
            mixed += acc_old[:, lanes] * rescale
        acc[:, lanes] = mixed
        top_out[0:1, lanes] = best
        total[0:1, lanes] = sums


def cached_kernel(lengths, offsets, owners, queries, kv_x0, kv_x1, *rest, late):
    acc, top, total, scores, maxima = rest[-5:]
    acc_old, top_old, total_old = rest[:3] if late else (None, None, None)
    z, x, _, _ = coordinates()
    length, offset, owner = [ref[z >> 1] for ref in (lengths, offsets, owners)]
    maxima[...] = jnp.full(maxima.shape, FLOOR, F32)
    lane = lax.broadcasted_iota(jnp.int32, (1, 256), 1)
    token = (lane // 128 * 2 + x) * 128 + lane % 128
    oldest = length + token - WIN
    place = 2 * (z & 1) + x
    for shard, (flip, source) in enumerate(((2 * late, kv_x0), (2 * late + 1, kv_x1))):
        begin = (((place ^ flip) - owner) & (GROUP - 1)) * 1024 - offset + length
        for chunk in range(1024 // CHUNK):
            first = (begin + chunk * CHUNK) & (WIN - 1)
            last = first + CHUNK - 1
            whole = (last < length) & (last < WIN) & (first > length + NEW - 1 - WIN)
            keys = source[0:80, chunk * CHUNK : (chunk + 1) * CHUNK]
            row = shard * 1024 + chunk * CHUNK

            @pl.when(whole)
            def _(keys=keys, row=row):
                score(keys, queries, None, scores, row, maxima)

            @pl.when(jnp.logical_not(whole))
            def _(keys=keys, row=row, first=first):
                slot = lax.broadcasted_iota(jnp.int32, (CHUNK, 128), 0)
                position = (first + slot) & (WIN - 1)
                position = jnp.where(position < length, position, -2 * WIN)
                allowed = jnp.concatenate([position, position], axis=1) > oldest
                score(keys, queries, allowed, scores, row, maxima)

    def values_of(first):
        source = (kv_x0, kv_x1)[first // 1024]
        return source[80:160, first % 1024 : first % 1024 + CHUNK]

    weigh(
        scores, values_of, CHUNK, maxima, top_old, acc_old, total_old, acc, top, total
    )


def fresh_kernel(
    queries, kv_mine, kv_other, acc_old, top_old, total_old, out, acc, top, total, scores, maxima
):
    _, x, _, _ = coordinates()
    maxima[...] = jnp.full(maxima.shape, FLOOR, F32)
    lane = lax.broadcasted_iota(jnp.int32, (1, 256), 1)
    token = (lane // 128 * 2 + x) * 128 + lane % 128
    for index, (source, its_x) in enumerate(((kv_mine, x), (kv_other, 1 - x))):
        row = lax.broadcasted_iota(jnp.int32, (256, 256), 0)
        key_token = (row // 128 * 2 + its_x) * 128 + row % 128
        score(source[0:80, 0:256], queries, key_token <= token, scores, index * 256, maxima)

    def values_of(first):
        return (kv_mine, kv_other)[first // 256][80:160, 0:256]

    weigh(scores, values_of, 256, maxima, top_old, acc_old, total_old, acc, top, total)
    for head in range(4):
        lanes = slice(head * 256, (head + 1) * 256)
        out[head * 80 : (head + 1) * 80] = (acc[:, lanes] / total[0:1, lanes]).astype(BF16)


def append_kernel(
    offsets, owners, kv_mine, kv_other, kv_z, cache_keys, cache_values, put_keys, put_values, fresh
):
    z, x, _, _ = coordinates()
    zz = z & 1
    offset, owner = offsets[z >> 1], owners[z >> 1]
    first = ((2 * zz + x - owner) & (GROUP - 1)) * 1024
    upper = x == 1
    for head, (mine, other) in enumerate(((kv_mine, kv_other), (kv_z.at[0], kv_z.at[1]))):
        mine = mine[:, 0:256].astype(F32)
        other = other[:, 0:256].astype(F32)
        low = jnp.where(upper, other, mine)
        high = jnp.where(upper, mine, other)
        fresh[head, :, 0:128] = low[:, 0:128]
        fresh[head, :, 128:256] = high[:, 0:128]
        fresh[head, :, 256:384] = low[:, 128:256]
        fresh[head, :, 384:512] = high[:, 128:256]
        fresh[head, :, 512:1024] = jnp.zeros((160, 512), F32)
    shift = (offset - first) & 1023
    column = lax.broadcasted_iota(jnp.int32, (80, 1024), 1)
    written = ((column + first - offset) & (WIN - 1)) < 512
    for head in range(2):
        rows = slice(head * 80, (head + 1) * 80)
        moved = pltpu.roll(fresh[zz ^ head], shift, 1)
        put_keys[rows] = jnp.where(written, moved[0:80], cache_keys[rows].astype(F32)).astype(BF16)
        put_values[rows] = jnp.where(
            written, moved[80:160], cache_values[rows].astype(F32)
        ).astype(BF16)


def output_kernel(
    own, from_core, from_y, from_yc, mine_0, mine_1, mine_2, mine_3, far_0, far_1, far_2, far_3,
    out, heads, *, keep
):
    z, x, y, core = coordinates()
    narrow = 2 * y + core
    tokens = pl.ds(pl.multiple_of(((z & 1) ^ (1 - keep)) * 128, 128), 128)
    for step, source in enumerate((own, from_core, from_y, from_yc)):
        heads[step] = source[:, tokens]
    first = pl.multiple_of(jnp.where((z & 1) == x, 0, 160), 32)
    second = pl.multiple_of(jnp.where((z & 1) == x, 160, 0), 32)
    total = jnp.zeros((128, 640), F32)
    for i, (mine, far) in enumerate(
        ((mine_0, far_0), (mine_1, far_1), (mine_2, far_2), (mine_3, far_3))
    ):
        step = (z ^ i) ^ narrow
        lanes = slice(1024, 1664) if i == 0 else slice(256, 896) if i == 2 else slice(0, 640)
        for start, rows in ((first, mine[...]), (second, far[:, lanes])):
            total += lax.dot_general(
                heads[step, pl.ds(start, 160)],
                rows,
                (((0,), (0,)), ((), ())),
                preferred_element_type=F32,
            )
    out[...] = total.astype(out.dtype)


def shards_cube(
    tokens_in,
    norm_gain,
    query_weight,
    key_weight,
    value_weight,
    out_weight,
    cache_keys,
    cache_values,
    cached_len,
    append_slot,
    shard_owner,
):
    def flip_z(z, x, y, c):
        return (z ^ 1, x, y, c)

    def flip_x(z, x, y, c):
        return (z, 1 - x, y, c)

    def flip_y(z, x, y, c):
        return (z, x, 1 - y, c)

    def flip_core(z, x, y, c):
        return (z, x, y, 1 - c)

    def flip_half(z, x, y, c):
        return (z ^ 2, x, y, c)

    crossed = send(tokens_in, lambda z, x, y, c: (z ^ 2, x, 1 - y, c) if y != z // 2 else None)
    out_swapped = send(out_weight[160:320], flip_x)
    w_keep, w_give = call(
        pack_weights_kernel,
        (shaped((320, 480)), shaped((320, 480))),
        query_weight,
        key_weight.T,
        value_weight.T,
    )
    w_z = send(w_give, flip_z)
    w_keep_x = send(w_keep, flip_x)
    kv_own, kv_give, squares = call(
        pack_cache_kernel,
        (shaped((160, 1024)), shaped((160, 1024)), shaped((8, 128), F32)),
        tokens_in,
        cache_keys,
        cache_values,
    )
    half = lax.axis_index("wide") // 4
    x = lax.axis_index("wide") % 2
    lane = jnp.arange(256, dtype=jnp.int32)
    length = jnp.where(half == 0, cached_len[0], cached_len[1])
    position = length + (lane // 128 * 2 + x) * 128 + lane % 128
    inverse = ROPE_BASE ** (-(jnp.arange(40, dtype=F32) * (2.0 / HEAD_DIM)))
    angles = position.astype(F32)[None, :] * inverse[:, None]
    cos, sin = jnp.cos(angles), jnp.sin(angles)
    gain = norm_gain.astype(F32).reshape(2, 2, 640)

    squares_z2 = send(squares, flip_half)
    current = call(
        current_kernel, shaped((144, 640)), tokens_in, crossed, squares, squares_z2
    )
    current, w_z, w_keep_x, kv_own, kv_give = lax.optimization_barrier(
        (current, w_z, w_keep_x, kv_own, kv_give)
    )
    from_z = send(current, flip_z)
    from_y = send(current, flip_y)
    from_zy = send(from_z, flip_y)
    w_z_x = send(w_z, flip_x)
    piece_0, piece_there, kv_joined = call(
        pieces_kernel,
        (shaped((160, 640)), shaped((160, 640)), shaped((160, 1664))),
        out_weight,
        out_swapped,
        kv_own,
    )
    blocks = jnp.stack([current, from_z, from_y, from_zy])
    piece_2 = send(piece_0, flip_half)
    blocks, cos, sin, gain = lax.optimization_barrier((blocks, cos, sin, gain))
    other = send(blocks, flip_core)
    w_rows = call(
        assemble_kernel,
        shaped((640, 512)),
        w_keep,
        after(w_keep_x, from_z),
        flops=6000000000,
    )
    w_rows_z = call(assemble_kernel, shaped((640, 512)), w_z, w_z_x, flops=11000000000)
    kv_z = send(after(kv_give, other), flip_z)
    kv_own_x = send(after(kv_joined, w_rows_z), flip_x)


    own_sum, give_sum = call(
        project_kernel,
        (shaped((480, 256), F32), shaped((480, 256))),
        gain,
        current,
        from_z,
        from_y,
        from_zy,
        after(other, piece_2),
        w_rows,
        w_rows_z,
    )
    got_sum = send(give_sum, flip_half)
    piece_1 = send(after(piece_there, kv_z, give_sum), flip_z)
    piece_3 = send(after(piece_there, kv_z, give_sum), lambda z, x, y, c: (z ^ 3, x, y, c))
    got_sum = after(got_sum, kv_z, kv_own_x)
    kv_z_x = send(after(kv_z, give_sum), flip_x)

    queries, new_kv = call(
        rotary_kernel,
        (shaped((80, 1024)), shaped((160, 896))),
        own_sum,
        got_sum,
        cos,
        sin,
        piece_2,
        flops=2_500_000_000,
    )
    new_kv_x = send(new_kv, flip_x)

    scalars = (cached_len, append_slot, shard_owner)
    states = (shaped((80, 1024), F32), shaped((8, 1024), F32), shaped((8, 1024), F32))
    scratch = [pltpu.VMEM((2048, 1024), F32), pltpu.VMEM((8, 1024), F32)]
    state = call(
        functools.partial(cached_kernel, late=0),
        states,
        *scalars,
        queries,
        kv_own,
        kv_own_x,
        scalars=3,
        scratch=scratch,
    )
    state = call(
        functools.partial(cached_kernel, late=1),
        states,
        *scalars,
        queries,
        kv_z,
        kv_z_x,
        *state,
        scalars=3,
        scratch=scratch,
    )
    piece_1, piece_3 = after((piece_1, piece_3), state)
    far_13 = send(call(stack_kernel, shaped((2, 160, 640)), piece_1, piece_3), flip_x)
    attended = call(
        fresh_kernel,
        shaped((320, 256)),
        queries,
        new_kv,
        new_kv_x,
        *state,
        scratch=[
            pltpu.VMEM((80, 1024), F32),
            pltpu.VMEM((8, 1024), F32),
            pltpu.VMEM((8, 1024), F32),
            pltpu.VMEM((512, 1024), F32),
            pltpu.VMEM((8, 1024), F32),
        ],
    )

    new_kv_z = send(after(jnp.stack([new_kv[:, :256], new_kv_x[:, :256]]), attended), flip_z)
    from_core = send(attended, flip_core)
    from_y = send(attended, flip_y)
    from_yc = send(from_y, flip_core)
    operands = (
        attended,
        from_core,
        from_y,
        after(from_yc, new_kv_z),
        piece_0,
        piece_1,
        piece_2,
        piece_3,
        kv_own_x,
        far_13[0],
        new_kv_x,
        far_13[1],
    )
    give, keep = [
        call(
            functools.partial(output_kernel, keep=keep),
            shaped((128, 640), F32 if keep else BF16),
            *operands,
            scratch=[pltpu.VMEM((4, 320, 128), BF16)],
        )
        for keep in (0, 1)
    ]
    got = send(give, flip_z)
    put_keys, put_values = call(
        append_kernel,
        (shaped((160, 1024)), shaped((160, 1024))),
        append_slot,
        shard_owner,
        new_kv,
        new_kv_x,
        after(new_kv_z, give),
        cache_keys,
        cache_values,
        scalars=2,
        scratch=[pltpu.VMEM((2, 160, 1024), F32)],
    )
    update = (keep + got.astype(F32)).astype(BF16)
    return (update, put_keys, put_values)


def solution(mesh):
    in_specs = (
        P("wide", "narrow"),
        P(),
        P("wide", "narrow"),
        P("wide", "narrow"),
        P("wide", "narrow"),
        P("wide", "narrow"),
        P("narrow", "wide"),
        P("narrow", "wide"),
        P(),
        P(),
        P(),
    )
    out_specs = (P("wide", "narrow"), P("narrow", "wide"), P("narrow", "wide"))
    cube = dict(mesh.shape) == {"wide": 8, "narrow": 4}
    shards = shards_cube if cube else shards_any
    return jax.shard_map(shards, mesh=mesh, in_specs=in_specs, out_specs=out_specs, check_vma=False)
```

```python
import functools
import math

import jax
import jax.numpy as jnp
from jax import lax
from jax.experimental import pallas as pl
from jax.experimental.pallas import tpu as pltpu
from jax.sharding import PartitionSpec as P

HEAD_DIM = 80
WIN = 4096
GROUP_BITS = 2
GROUP = 4


EPSILON = 1e-05
ROPE_BASE = 10000.0
LOWEST = -1e30


def from_partner(block, axis, bit):
    count = lax.axis_size(axis)
    route = []
    for low in range(count):
        high = low | 1 << bit
        if high != low and high < count:
            route += [(low, high), (high, low)]
    return lax.ppermute(block, axis, route)


def rms_normed(rows_in, gain):
    values = rows_in.astype(jnp.float32)
    scaling = lax.rsqrt(jnp.mean(values * values, axis=-1, keepdims=True) + EPSILON)
    return (values * scaling * gain.astype(jnp.float32)).astype(jnp.bfloat16)


def rotate(values, positions):
    half_dim = values.shape[-1] // 2
    inverse = ROPE_BASE ** (-(jnp.arange(half_dim, dtype=jnp.float32) * (2.0 / values.shape[-1])))
    angles = positions.astype(jnp.float32)[:, None] * inverse[None, :]
    cos_part = jnp.cos(angles)[:, None, :]
    sin_part = jnp.sin(angles)[:, None, :]
    lower = values[..., :half_dim]
    higher = values[..., half_dim:]
    return jnp.concatenate(
        [lower * cos_part - higher * sin_part, higher * cos_part + lower * sin_part], axis=-1
    )


def ordered(mine, other, upper, along):
    first_half = jnp.where(upper, other, mine)
    second_half = jnp.where(upper, mine, other)
    return jnp.concatenate([first_half, second_half], axis=along)


def empty_state(row_count, groups, repeats):
    return (
        jnp.zeros((row_count, groups, repeats, HEAD_DIM), jnp.float32),
        jnp.full((row_count, groups, repeats), LOWEST, jnp.float32),
        jnp.zeros((row_count, groups, repeats), jnp.float32),
    )


def fold_keys(state, queries, query_pos, keys, values, key_pos, key_ok, widest):
    key_count = keys.shape[1]
    groups = queries.shape[1]
    block = math.gcd(key_count, widest)
    keys_split = keys.reshape(groups, HEAD_DIM, key_count)
    values_split = values.reshape(groups, HEAD_DIM, key_count)
    scale = HEAD_DIM ** (-0.5)

    def step(index, carry):
        accum, top_old, sum_old = carry
        start = index * block
        block_keys = lax.dynamic_slice_in_dim(keys_split, start, block, 2)
        block_values = lax.dynamic_slice_in_dim(values_split, start, block, 2)
        block_pos = lax.dynamic_slice_in_dim(key_pos, start, block, 0)
        block_ok = lax.dynamic_slice_in_dim(key_ok, start, block, 0)
        scores = (
            jnp.einsum("tgrd,gdk->tgrk", queries, block_keys, preferred_element_type=jnp.float32)
            * scale
        )
        allowed = (
            block_ok[None, :]
            & (block_pos[None, :] <= query_pos[:, None])
            & (query_pos[:, None] - block_pos[None, :] < WIN)
        )
        allowed = allowed[:, None, None, :]
        top_new = jnp.maximum(top_old, jnp.max(jnp.where(allowed, scores, LOWEST), axis=-1))
        weights = jnp.where(allowed, jnp.exp(scores - top_new[..., None]), 0.0)
        rescale = jnp.exp(top_old - top_new)
        sum_new = sum_old * rescale + jnp.sum(weights, axis=-1)
        mixed = jnp.einsum(
            "tgrk,gdk->tgrd",
            weights.astype(jnp.bfloat16),
            block_values,
            preferred_element_type=jnp.float32,
        )
        return (accum * rescale[..., None] + mixed, top_new, sum_new)

    return lax.fori_loop(0, key_count // block, step, state)


def shards_any(
    tokens_in,
    norm_gain,
    query_weight,
    key_weight,
    value_weight,
    out_weight,
    cache_keys,
    cache_values,
    cached_len,
    append_slot,
    shard_owner,
):
    whole = lax.all_gather(tokens_in, "narrow", axis=1, tiled=True)
    normed = rms_normed(whole, norm_gain)
    tok_rows = whole.shape[0]
    query_width = query_weight.shape[1]
    kv_width = key_weight.shape[1]
    local_heads = query_width // HEAD_DIM
    local_groups = kv_width // HEAD_DIM
    repeats = local_heads // local_groups
    columns = normed
    query_sum = jnp.dot(
        columns,
        lax.all_gather(query_weight, "wide", axis=0, tiled=True),
        preferred_element_type=jnp.float32,
    )
    key_sum = jnp.dot(
        columns,
        lax.all_gather(key_weight, "wide", axis=0, tiled=True),
        preferred_element_type=jnp.float32,
    )
    value_sum = jnp.dot(
        columns,
        lax.all_gather(value_weight, "wide", axis=0, tiled=True),
        preferred_element_type=jnp.float32,
    )
    position = lax.axis_index("wide")
    request = position // GROUP
    place = position % GROUP
    length = cached_len[request]
    offset = append_slot[request]
    owner = shard_owner[request]
    query_pos = length + place * tok_rows + jnp.arange(tok_rows, dtype=jnp.int32)
    queries = rotate(query_sum.reshape(tok_rows, local_heads, HEAD_DIM), query_pos).astype(
        jnp.bfloat16
    )
    queries = queries.reshape(tok_rows, local_groups, repeats, HEAD_DIM)
    new_keys = (
        rotate(key_sum.reshape(tok_rows, local_groups, HEAD_DIM), query_pos)
        .astype(jnp.bfloat16)
        .reshape(tok_rows, kv_width)
    )
    new_values = value_sum.astype(jnp.bfloat16)
    shard_rows = cache_keys.shape[1]
    within = jnp.arange(shard_rows, dtype=jnp.int32)
    cycle_mine = (place - owner) % GROUP * shard_rows + within
    old_keys, old_values = (cache_keys, cache_values)
    for bit in range(GROUP_BITS):
        upper = place // 2**bit % 2 == 1
        other_keys, other_values, other_old_keys, other_old_values = from_partner(
            (new_keys, new_values, old_keys, old_values), "wide", bit
        )
        new_keys = ordered(new_keys, other_keys, upper, 0)
        new_values = ordered(new_values, other_values, upper, 0)
        old_keys = ordered(old_keys, other_old_keys, upper, 1)
        old_values = ordered(old_values, other_old_values, upper, 1)
    slot_index = jnp.arange(old_keys.shape[1], dtype=jnp.int32)
    cycle = (slot_index // shard_rows - owner) % GROUP * shard_rows + slot_index % shard_rows
    cached_pos = (cycle - offset + length) % WIN
    state = fold_keys(
        empty_state(tok_rows, local_groups, repeats),
        queries,
        query_pos,
        old_keys,
        old_values,
        cached_pos,
        cached_pos < length,
        512,
    )
    key_cols = new_keys.T
    value_cols = new_values.T
    new_count = key_cols.shape[1]
    new_pos = length + jnp.arange(new_count, dtype=jnp.int32)
    state = fold_keys(
        state,
        queries,
        query_pos,
        key_cols,
        value_cols,
        new_pos,
        jnp.ones((new_count,), dtype=bool),
        512,
    )
    accum, top_score, total = state
    attended = (accum / total[..., None]).astype(jnp.bfloat16).reshape(tok_rows, query_width)
    all_heads = lax.all_gather(attended, "narrow", axis=1, tiled=True)
    columns = all_heads
    update = jnp.dot(
        columns,
        lax.all_gather(out_weight, "wide", axis=0, tiled=True),
        preferred_element_type=jnp.float32,
    ).astype(jnp.bfloat16)
    new_index = (cycle_mine - offset) % WIN
    written = new_index < new_count
    take_rows = jnp.minimum(new_index, new_count - 1)
    put_keys = jnp.where(written[None, :], jnp.take(key_cols, take_rows, axis=1), cache_keys)
    put_values = jnp.where(written[None, :], jnp.take(value_cols, take_rows, axis=1), cache_values)
    return (update, put_keys, put_values)


F32 = jnp.float32
BF16 = jnp.bfloat16
MASKED = -1e30
FLOOR = -1e29
EXP2_SCALE = HEAD_DIM ** (-0.5) * math.log2(math.e)
CHUNK = 512
NEW = 512


def send(block, to):
    route = []
    for z in range(4):
        for x in range(2):
            for y in range(2):
                for c in range(2):
                    there = to(z, x, y, c)
                    if there is not None:
                        tz, tx, ty, tc = there
                        route.append(((2 * z + x) * 4 + 2 * y + c, (2 * tz + tx) * 4 + 2 * ty + tc))
    return lax.ppermute(block, ("wide", "narrow"), route)


def after(block, *earlier):
    return lax.optimization_barrier((block, *earlier))[0]


def call(kernel, outs, *args, scalars=0, scratch=(), flops=1, space=pltpu.VMEM, room=40):
    specs = [pl.BlockSpec(memory_space=pltpu.SMEM)] * scalars
    specs += [pl.BlockSpec(memory_space=space)] * (len(args) - scalars)
    return pl.pallas_call(
        kernel,
        out_shape=outs,
        in_specs=specs,
        out_specs=jax.tree.map(lambda _: pl.BlockSpec(memory_space=pltpu.VMEM), outs),
        scratch_shapes=scratch,
        compiler_params=pltpu.CompilerParams(vmem_limit_bytes=room * 1024 * 1024),
        cost_estimate=pl.CostEstimate(flops=flops, bytes_accessed=1, transcendentals=0),
    )(*args)


def shaped(shape, kind=BF16):
    return jax.ShapeDtypeStruct(shape, kind)


def coordinates():
    wide = lax.axis_index("wide")
    narrow = lax.axis_index("narrow")
    return wide >> 1, wide & 1, narrow >> 1, narrow & 1


def pack_weights_kernel(wq_far, wk_far, wv_far, w_keep, w_give, wq, wk, wv, arrived):
    copies = [
        pltpu.make_async_copy(source, target, arrived.at[index])
        for index, (source, target) in enumerate(((wq_far, wq), (wk_far, wk), (wv_far, wv)))
    ]
    for copy in copies:
        copy.start()
    for copy in copies:
        copy.wait()
    z, _, _, _ = coordinates()
    zz = z & 1
    for group in range(2):

        def fill(weights, group=group):
            weights[:, 0:320] = wq[:, 320 * group : 320 * (group + 1)]
            weights[:, 320:400] = wk[80 * group : 80 * (group + 1)].T
            weights[:, 400:480] = wv[80 * group : 80 * (group + 1)].T

        @pl.when(zz == group)
        def _(fill=fill):
            fill(w_keep)

        @pl.when(zz != group)
        def _(fill=fill):
            fill(w_give)


def pack_cache_kernel(tokens, keys, values, kv_own, kv_give, squares):
    z, _, _, _ = coordinates()
    zz = z & 1
    for group in range(2):

        def fill(cache, group=group):
            cache[0:80] = keys[80 * group : 80 * (group + 1)]
            cache[80:160] = values[80 * group : 80 * (group + 1)]

        @pl.when(zz == group)
        def _(fill=fill):
            fill(kv_own)

        @pl.when(zz != group)
        def _(fill=fill):
            fill(kv_give)

    wide_tokens = tokens[...].astype(F32)
    total = jnp.sum(wide_tokens * wide_tokens, axis=1, keepdims=True)
    squares[...] = jnp.broadcast_to(total, (128, 128)).T[0:8]


def current_kernel(tokens, crossed, squares, squares_z2, out):
    z, _, y, _ = coordinates()
    at_home = y == z >> 1

    @pl.when(at_home)
    def _():
        out[0:128] = tokens[...]

    @pl.when(jnp.logical_not(at_home))
    def _():
        out[0:128] = crossed[...]

    out[128:144] = jnp.zeros((16, 640), BF16)
    row = lax.broadcasted_iota(jnp.int32, (16, 128), 0)
    rest = jnp.where(
        row == 0,
        jnp.concatenate([squares[...]] * 2, axis=0),
        jnp.where(row == 1, jnp.concatenate([squares_z2[...]] * 2, axis=0), 0.0),
    )
    for part in range(3):
        rounded = rest.astype(BF16)
        rest = rest - rounded.astype(F32)
        out[128:144, 128 * part : 128 * (part + 1)] = rounded


def pieces_kernel(weight, swapped, kv_own, here, there, joined):
    z, x, _, _ = coordinates()
    same = (z & 1) == x

    @pl.when(same)
    def _():
        here[...] = weight[0:160]
        there[...] = swapped[...]

    @pl.when(jnp.logical_not(same))
    def _():
        here[...] = swapped[...]
        there[...] = weight[0:160]

    joined[:, 0:1024] = kv_own[...]
    joined[:, 1024:1664] = here[...]


def assemble_kernel(near, far, out):
    _, x, _, _ = coordinates()
    depth = near.shape[0]
    out[pl.ds(pl.multiple_of(x * depth, 64), depth), 0:480] = near[...]
    out[pl.ds(pl.multiple_of((1 - x) * depth, 64), depth), 0:480] = far[...]
    out[:, 480:] = jnp.zeros((2 * depth, 32), BF16)


def stack_kernel(first, second, out):
    out[0] = first[...]
    out[1] = second[...]


def project_kernel(
    gain, current, from_z, from_y, from_zy, other, w_rows, w_rows_z,
    own_out, send_out
):
    z, x, y, core = coordinates()
    half, zz = z >> 1, z & 1
    at_home = y == half
    here = zz == core
    w_here = jnp.where(here, w_rows[...], w_rows_z[...])
    w_there = jnp.where(here, w_rows_z[...], w_rows[...])
    both = gain[pl.ds(half, 1)][0]
    swap = core == 1
    gain_here = jnp.where(swap, both[1:2], both[0:1])
    gain_there = jnp.where(swap, both[0:1], both[1:2])

    def stats(block):
        rows = block[128:144].astype(F32)
        return rows[:, 0:128] + rows[:, 128:256] + rows[:, 256:384]

    def scaling_of(blocks):
        total = sum(stats(block) for block in blocks)
        scale = lax.rsqrt(total / 2560.0 + EPSILON)
        return jnp.concatenate([scale] * 8, axis=0).T

    scale_z = scaling_of((current, from_y, other.at[0], other.at[2]))
    scale_z1 = scaling_of((from_z, from_zy, other.at[1], other.at[3]))

    def product(here, there, scale):
        normed_here = (here[0:128].astype(F32) * scale * gain_here).astype(BF16)
        normed_there = (there[0:128].astype(F32) * scale * gain_there).astype(BF16)
        total = jnp.dot(normed_here, w_here, preferred_element_type=F32)
        total += jnp.dot(normed_there, w_there, preferred_element_type=F32)
        return total.T[0:480]

    def products(first, second, row, out):
        for (here, there), scaling, place in (
            (first, scale_z[:, row : row + 1], zz),
            (second, scale_z1[:, row : row + 1], 1 - zz),
        ):
            result = product(here, there, scaling)
            lanes = pl.ds(pl.multiple_of(place * 128, 128), 128)
            out[:, lanes] = result.astype(out.dtype)

    first = ((current, other.at[0]), (from_z, other.at[1]))
    second = ((from_y, other.at[2]), (from_zy, other.at[3]))

    @pl.when(at_home)
    def _():
        products(*second, 1, send_out)
        products(*first, 0, own_out)

    @pl.when(jnp.logical_not(at_home))
    def _():
        products(*first, 1, send_out)
        products(*second, 0, own_out)


def rotary_kernel(own, received, cos, sin, piece_2, q_out, kv_out):
    total = own[...] + received[...].astype(F32)
    cos_part = cos[...]
    sin_part = sin[...]
    rows = own.shape[1]

    def rotated(first):
        lower = total[first : first + 40]
        higher = total[first + 40 : first + 80]
        return jnp.concatenate(
            [lower * cos_part - higher * sin_part, higher * cos_part + lower * sin_part], axis=0
        ).astype(BF16)

    for head in range(4):
        q_out[:, head * rows : (head + 1) * rows] = rotated(80 * head)
    kv_out[0:80, 0:256] = rotated(320)
    kv_out[80:160, 0:256] = total[400:480].astype(BF16)
    kv_out[:, 256:896] = piece_2[...]


def score(keys, queries, allowed, scores, first, top):
    turned = keys.T
    count = turned.shape[0]
    for head in range(4):
        lanes = slice(head * 256, (head + 1) * 256)
        part = jnp.dot(turned, queries[:, lanes], preferred_element_type=F32) * EXP2_SCALE
        if allowed is not None:
            part = jnp.where(allowed, part, MASKED)
        scores[first : first + count, lanes] = part
        top[:, lanes] = jnp.maximum(
            top[:, lanes], jnp.max(part.reshape(count // 8, 8, 256), axis=0)
        )


def weigh(scores, values_of, block, top, top_old, acc_old, total_old, acc, top_out, total):
    count = scores.shape[0]
    for head in range(4):
        lanes = slice(head * 256, (head + 1) * 256)
        best = jnp.max(top[:, lanes], axis=0, keepdims=True)
        if top_old is not None:
            best = jnp.maximum(best, top_old[0:1, lanes])
        sums = jnp.zeros((8, 256), F32)
        mixed = jnp.zeros((80, 256), F32)
        for first in range(0, count, block):
            weights = jnp.exp2(scores[first : first + block, lanes] - best)
            sums += jnp.sum(weights.reshape(block // 8, 8, 256), axis=0)
            mixed += jnp.dot(
                values_of(first), weights.astype(BF16), preferred_element_type=F32
            )
        sums = jnp.sum(sums, axis=0, keepdims=True)
        if top_old is not None:
            rescale = jnp.exp2(top_old[0:1, lanes] - best)
            sums += total_old[0:1, lanes] * rescale
            mixed += acc_old[:, lanes] * rescale
        acc[:, lanes] = mixed
        top_out[0:1, lanes] = best
        total[0:1, lanes] = sums


def cached_kernel(lengths, offsets, owners, queries, kv_x0, kv_x1, *rest, late):
    acc, top, total, scores, maxima = rest[-5:]
    acc_old, top_old, total_old = rest[:3] if late else (None, None, None)
    z, x, _, _ = coordinates()
    length, offset, owner = [ref[z >> 1] for ref in (lengths, offsets, owners)]
    maxima[...] = jnp.full(maxima.shape, FLOOR, F32)
    lane = lax.broadcasted_iota(jnp.int32, (1, 256), 1)
    token = (lane // 128 * 2 + x) * 128 + lane % 128
    oldest = length + token - WIN
    place = 2 * (z & 1) + x
    for shard, (flip, source) in enumerate(((2 * late, kv_x0), (2 * late + 1, kv_x1))):
        begin = (((place ^ flip) - owner) & (GROUP - 1)) * 1024 - offset + length
        for chunk in range(1024 // CHUNK):
            first = (begin + chunk * CHUNK) & (WIN - 1)
            last = first + CHUNK - 1
            whole = (last < length) & (last < WIN) & (first > length + NEW - 1 - WIN)
            keys = source[0:80, chunk * CHUNK : (chunk + 1) * CHUNK]
            row = shard * 1024 + chunk * CHUNK

            @pl.when(whole)
            def _(keys=keys, row=row):
                score(keys, queries, None, scores, row, maxima)

            @pl.when(jnp.logical_not(whole))
            def _(keys=keys, row=row, first=first):
                slot = lax.broadcasted_iota(jnp.int32, (CHUNK, 128), 0)
                position = (first + slot) & (WIN - 1)
                position = jnp.where(position < length, position, -2 * WIN)
                allowed = jnp.concatenate([position, position], axis=1) > oldest
                score(keys, queries, allowed, scores, row, maxima)

    def values_of(first):
        source = (kv_x0, kv_x1)[first // 1024]
        return source[80:160, first % 1024 : first % 1024 + CHUNK]

    weigh(
        scores, values_of, CHUNK, maxima, top_old, acc_old, total_old, acc, top, total
    )


def fresh_kernel(
    queries, kv_mine, kv_other, acc_old, top_old, total_old, out, acc, top, total, scores, maxima
):
    _, x, _, _ = coordinates()
    maxima[...] = jnp.full(maxima.shape, FLOOR, F32)
    lane = lax.broadcasted_iota(jnp.int32, (1, 256), 1)
    token = (lane // 128 * 2 + x) * 128 + lane % 128
    for index, (source, its_x) in enumerate(((kv_mine, x), (kv_other, 1 - x))):
        row = lax.broadcasted_iota(jnp.int32, (256, 256), 0)
        key_token = (row // 128 * 2 + its_x) * 128 + row % 128
        score(source[0:80, 0:256], queries, key_token <= token, scores, index * 256, maxima)

    def values_of(first):
        return (kv_mine, kv_other)[first // 256][80:160, 0:256]

    weigh(scores, values_of, 256, maxima, top_old, acc_old, total_old, acc, top, total)
    for head in range(4):
        lanes = slice(head * 256, (head + 1) * 256)
        out[head * 80 : (head + 1) * 80] = (acc[:, lanes] / total[0:1, lanes]).astype(BF16)


def append_kernel(
    offsets, owners, kv_mine, kv_other, kv_z, cache_keys, cache_values, put_keys, put_values, fresh
):
    z, x, _, _ = coordinates()
    zz = z & 1
    offset, owner = offsets[z >> 1], owners[z >> 1]
    first = ((2 * zz + x - owner) & (GROUP - 1)) * 1024
    upper = x == 1
    for head, (mine, other) in enumerate(((kv_mine, kv_other), (kv_z.at[0], kv_z.at[1]))):
        mine = mine[:, 0:256].astype(F32)
        other = other[:, 0:256].astype(F32)
        low = jnp.where(upper, other, mine)
        high = jnp.where(upper, mine, other)
        fresh[head, :, 0:128] = low[:, 0:128]
        fresh[head, :, 128:256] = high[:, 0:128]
        fresh[head, :, 256:384] = low[:, 128:256]
        fresh[head, :, 384:512] = high[:, 128:256]
        fresh[head, :, 512:1024] = jnp.zeros((160, 512), F32)
    shift = (offset - first) & 1023
    column = lax.broadcasted_iota(jnp.int32, (80, 1024), 1)
    written = ((column + first - offset) & (WIN - 1)) < 512
    for head in range(2):
        rows = slice(head * 80, (head + 1) * 80)
        moved = pltpu.roll(fresh[zz ^ head], shift, 1)
        put_keys[rows] = jnp.where(written, moved[0:80], cache_keys[rows].astype(F32)).astype(BF16)
        put_values[rows] = jnp.where(
            written, moved[80:160], cache_values[rows].astype(F32)
        ).astype(BF16)


def output_kernel(
    own, from_core, from_y, from_yc, mine_0, mine_1, mine_2, mine_3, far_0, far_1, far_2, far_3,
    out, heads, *, keep
):
    z, x, y, core = coordinates()
    narrow = 2 * y + core
    tokens = pl.ds(pl.multiple_of(((z & 1) ^ (1 - keep)) * 128, 128), 128)
    for step, source in enumerate((own, from_core, from_y, from_yc)):
        heads[step] = source[:, tokens]
    first = pl.multiple_of(jnp.where((z & 1) == x, 0, 160), 32)
    second = pl.multiple_of(jnp.where((z & 1) == x, 160, 0), 32)
    total = jnp.zeros((128, 640), F32)
    for i, (mine, far) in enumerate(
        ((mine_0, far_0), (mine_1, far_1), (mine_2, far_2), (mine_3, far_3))
    ):
        step = (z ^ i) ^ narrow
        lanes = slice(1024, 1664) if i == 0 else slice(256, 896) if i == 2 else slice(0, 640)
        for start, rows in ((first, mine[...]), (second, far[:, lanes])):
            total += lax.dot_general(
                heads[step, pl.ds(start, 160)],
                rows,
                (((0,), (0,)), ((), ())),
                preferred_element_type=F32,
            )
    out[...] = total.astype(out.dtype)


def shards_cube(
    tokens_in,
    norm_gain,
    query_weight,
    key_weight,
    value_weight,
    out_weight,
    cache_keys,
    cache_values,
    cached_len,
    append_slot,
    shard_owner,
):
    def flip_z(z, x, y, c):
        return (z ^ 1, x, y, c)

    def flip_x(z, x, y, c):
        return (z, 1 - x, y, c)

    def flip_y(z, x, y, c):
        return (z, x, 1 - y, c)

    def flip_core(z, x, y, c):
        return (z, x, y, 1 - c)

    def flip_half(z, x, y, c):
        return (z ^ 2, x, y, c)

    crossed = send(tokens_in, lambda z, x, y, c: (z ^ 2, x, 1 - y, c) if y != z // 2 else None)
    out_swapped = send(out_weight[160:320], flip_x)
    w_keep, w_give = call(
        pack_weights_kernel,
        (shaped((320, 480)), shaped((320, 480))),
        query_weight,
        key_weight.T,
        value_weight.T,
        space=pltpu.HBM,
        room=62,
        scratch=[
            pltpu.VMEM((320, 640), BF16),
            pltpu.VMEM((160, 320), BF16),
            pltpu.VMEM((160, 320), BF16),
            pltpu.SemaphoreType.DMA((3,)),
        ],
    )
    w_z = send(w_give, flip_z)
    w_keep_x = send(w_keep, flip_x)
    kv_own, kv_give, squares = call(
        pack_cache_kernel,
        (shaped((160, 1024)), shaped((160, 1024)), shaped((8, 128), F32)),
        tokens_in,
        cache_keys,
        cache_values,
    )
    half = lax.axis_index("wide") // 4
    x = lax.axis_index("wide") % 2
    lane = jnp.arange(256, dtype=jnp.int32)
    length = jnp.where(half == 0, cached_len[0], cached_len[1])
    position = length + (lane // 128 * 2 + x) * 128 + lane % 128
    inverse = ROPE_BASE ** (-(jnp.arange(40, dtype=F32) * (2.0 / HEAD_DIM)))
    angles = position.astype(F32)[None, :] * inverse[:, None]
    cos, sin = jnp.cos(angles), jnp.sin(angles)
    gain = norm_gain.astype(F32).reshape(2, 2, 640)

    squares_z2 = send(squares, flip_half)
    current = call(
        current_kernel, shaped((144, 640)), tokens_in, crossed, squares, squares_z2
    )
    current, w_z, w_keep_x, kv_own, kv_give = lax.optimization_barrier(
        (current, w_z, w_keep_x, kv_own, kv_give)
    )
    from_z = send(current, flip_z)
    from_y = send(current, flip_y)
    from_zy = send(from_z, flip_y)
    w_z_x = send(w_z, flip_x)
    piece_0, piece_there, kv_joined = call(
        pieces_kernel,
        (shaped((160, 640)), shaped((160, 640)), shaped((160, 1664))),
        out_weight,
        out_swapped,
        kv_own,
    )
    blocks = jnp.stack([current, from_z, from_y, from_zy])
    piece_2 = send(piece_0, flip_half)
    blocks, cos, sin, gain = lax.optimization_barrier((blocks, cos, sin, gain))
    other = send(blocks, flip_core)
    w_rows = call(
        assemble_kernel,
        shaped((640, 512)),
        w_keep,
        after(w_keep_x, from_z),
        flops=6000000000,
    )
    w_rows_z = call(assemble_kernel, shaped((640, 512)), w_z, w_z_x, flops=11000000000)
    kv_z = send(after(kv_give, from_z), flip_z)
    kv_own_x = send(after(kv_joined, w_rows_z), flip_x)


    own_sum, give_sum = call(
        project_kernel,
        (shaped((480, 256), F32), shaped((480, 256))),
        gain,
        current,
        from_z,
        from_y,
        from_zy,
        after(other, piece_2),
        w_rows,
        w_rows_z,
    )
    got_sum = send(give_sum, flip_half)
    got_sum = after(got_sum, kv_z, kv_own_x)
    kv_z_x = send(after(kv_z, give_sum), flip_x)

    queries, new_kv = call(
        rotary_kernel,
        (shaped((80, 1024)), shaped((160, 896))),
        own_sum,
        got_sum,
        cos,
        sin,
        piece_2,
        flops=2_500_000_000,
    )
    new_kv_x = send(new_kv, flip_x)
    piece_1 = send(after(piece_there, queries), flip_z)
    piece_3 = send(after(piece_there, queries), lambda z, x, y, c: (z ^ 3, x, y, c))

    scalars = (cached_len, append_slot, shard_owner)
    states = (shaped((80, 1024), F32), shaped((8, 1024), F32), shaped((8, 1024), F32))
    scratch = [pltpu.VMEM((2048, 1024), F32), pltpu.VMEM((8, 1024), F32)]
    state = call(
        functools.partial(cached_kernel, late=0),
        states,
        *scalars,
        queries,
        kv_own,
        kv_own_x,
        scalars=3,
        scratch=scratch,
    )
    state = call(
        functools.partial(cached_kernel, late=1),
        states,
        *scalars,
        queries,
        kv_z,
        kv_z_x,
        *state,
        scalars=3,
        scratch=scratch,
    )
    piece_1, piece_3 = after((piece_1, piece_3), state)
    far_13 = send(call(stack_kernel, shaped((2, 160, 640)), piece_1, piece_3), flip_x)
    attended = call(
        fresh_kernel,
        shaped((320, 256)),
        queries,
        new_kv,
        new_kv_x,
        *state,
        scratch=[
            pltpu.VMEM((80, 1024), F32),
            pltpu.VMEM((8, 1024), F32),
            pltpu.VMEM((8, 1024), F32),
            pltpu.VMEM((512, 1024), F32),
            pltpu.VMEM((8, 1024), F32),
        ],
    )

    new_kv_z = send(after(jnp.stack([new_kv[:, :256], new_kv_x[:, :256]]), attended), flip_z)
    from_core = send(attended, flip_core)
    from_y = send(attended, flip_y)
    from_yc = send(from_y, flip_core)
    operands = (
        attended,
        from_core,
        from_y,
        after(from_yc, new_kv_z),
        piece_0,
        piece_1,
        piece_2,
        piece_3,
        kv_own_x,
        far_13[0],
        new_kv_x,
        far_13[1],
    )
    give, keep = [
        call(
            functools.partial(output_kernel, keep=keep),
            shaped((128, 640), F32 if keep else BF16),
            *operands,
            scratch=[pltpu.VMEM((4, 320, 128), BF16)],
        )
        for keep in (0, 1)
    ]
    got = send(give, flip_z)
    put_keys, put_values = call(
        append_kernel,
        (shaped((160, 1024)), shaped((160, 1024))),
        append_slot,
        shard_owner,
        new_kv,
        new_kv_x,
        after(new_kv_z, give),
        cache_keys,
        cache_values,
        scalars=2,
        scratch=[pltpu.VMEM((2, 160, 1024), F32)],
    )
    update = (keep + got.astype(F32)).astype(BF16)
    return (update, put_keys, put_values)


def solution(mesh):
    in_specs = (
        P("wide", "narrow"),
        P(),
        P("wide", "narrow"),
        P("wide", "narrow"),
        P("wide", "narrow"),
        P("wide", "narrow"),
        P("narrow", "wide"),
        P("narrow", "wide"),
        P(),
        P(),
        P(),
    )
    out_specs = (P("wide", "narrow"), P("narrow", "wide"), P("narrow", "wide"))
    cube = dict(mesh.shape) == {"wide": 8, "narrow": 4}
    shards = shards_cube if cube else shards_any
    return jax.shard_map(shards, mesh=mesh, in_specs=in_specs, out_specs=out_specs, check_vma=False)
```
